32 devices in a mesh: layer: 8 (over z, y), rhs: 4 (over x, core).
Axes of the slice: x: 2, y: 2, z: 4, core: 2. Of those that a mesh axis runs over, the one named last changes fastest.
Arguments:
- coupling: float32 [8, 640, 640], P('layer', 'rhs'), may hold values from -8 to 12, as said below
- density: int32 [8, 640], P('layer'), may hold values 0 or 1
- support: float32 [8, 640], P('layer'), may hold values from 0.2 to 2
- loads: float32 [8, 640, 1024], P('layer', None, 'rhs'), may hold values from -6 to 6
Outputs:
- reduced_diag: float32 [8, 640, 640], P('layer', 'rhs')
- reduced_lower: float32 [8, 640, 640], P('layer', 'rhs')
- reduced_upper: float32 [8, 640, 640], P('layer', 'rhs')
- reduced_loads: float32 [8, 640, 1024], P('layer', None, 'rhs')
The draws below stay inside these ranges and needn't reach their ends.
Inputs may be any that keep to these rules, and one draw needn't show every extreme that they name: Each coupling block is symmetric and positive definite.
All inputs are finite; a program needn't handle non-finite values. No bound on the sum of `density` on one device may be relied on, other than what follows from the above.
Results may differ from the reference program's by a relative error of at most 0.0003.
Values sent between devices are 32-bit elements; how exact they have to be, the bound alone decides.
A program may use at most 64 MiB of HBM per device.

```python
import math
import jax
import jax.numpy as jnp
from jax import lax

M = 640
LEVELS = 2
LAYERS = 8
NRHS = 1024


def signed_gains(magnitude_key, sign_key, lo, hi):
    magnitude = jnp.exp(jax.random.uniform(magnitude_key, (LAYERS, M), jnp.float32, math.log(lo), math.log(hi)))
    signs = jnp.where(jax.random.bernoulli(sign_key, 0.5, (LAYERS, M)), jnp.float32(1.0), jnp.float32(-1.0))
    return magnitude * signs


def kernel_part(positions, gains, length):
    gap = jnp.abs(positions[:, :, None] - positions[:, None, :])
    return jnp.exp(-gap / length) * gains[:, :, None] * gains[:, None, :]


def draw_coupling(key, part):
    key = jax.random.fold_in(key, 11)
    keys = jax.random.split(key, 7)
    near_pos = jax.random.uniform(keys[0], (LAYERS, M), jnp.float32, 0.0, 1.0) * M
    far_pos = jax.random.uniform(keys[1], (LAYERS, M), jnp.float32, 0.0, 1.0) * M
    near_gain = signed_gains(keys[2], keys[3], 0.6, 1.6)
    far_gain = signed_gains(keys[4], keys[5], 0.6, 1.6)
    shift = jax.random.uniform(keys[6], (LAYERS, M), jnp.float32, 0.5, 1.5)
    identity = jnp.eye(M, dtype=jnp.float32)
    matrix = kernel_part(near_pos, near_gain, 4.0) + 0.5 * kernel_part(far_pos, far_gain, 16.0)
    matrix = matrix + shift[:, :, None] * identity
    return matrix


def plant(result, rng, low, top_value):
    place = [jax.random.randint(jax.random.fold_in(rng, axis), (), 0, length) for axis, length in enumerate(result.shape)]
    longest = result.shape.index(max(result.shape))
    beside = place[:longest] + [(place[longest] + 1) % result.shape[longest]] + place[longest + 1:]
    return result.at[tuple(place)].set(low).at[tuple(beside)].set(top_value)


def levels(rng, shape, shards, low, high):
    gain = 1.0
    for axis_at, shards_of in shards:
        steps = jax.random.uniform(jax.random.fold_in(jax.random.fold_in(rng, 6), axis_at), (shards_of,), jnp.float32, low / len(shards), high / len(shards))
        gain = gain * jnp.repeat(jnp.exp(steps), shape[axis_at] // shards_of).reshape((-1,) + (1,) * (len(shape) - 1 - axis_at))
    return gain


def scatter_about(own_key, extent, scale, bound, pieces=(), kind=jnp.bfloat16):
    values = jax.random.normal(own_key, extent, jnp.float32) * scale
    if len(pieces) > 0:
        values = levels(own_key, extent, pieces, -0.22, 0.18) * values
    return jnp.clip(values, min=-bound, max=bound).astype(kind)


def setup_inputs(seed: int = 0) -> dict:
    arg_keys = jax.random.split(jax.random.key(seed), 5)
    coupling = draw_coupling(jax.random.fold_in(arg_keys[4], 71), 0)
    density = plant((jax.random.randint(arg_keys[1], (LAYERS, M), 0, 4) < 3).astype(jnp.int32), jax.random.fold_in(arg_keys[1], 1), 0, 1)
    support = jnp.clip(jnp.exp(math.log(2.0) - 2.3025851 * jax.random.uniform(arg_keys[2], (LAYERS, M), jnp.float32) ** levels(arg_keys[2], (LAYERS, M), ((0, 8),), -0.2, 0.2)), 0.2, 2.0)
    loads = scatter_about(arg_keys[3], (LAYERS, M, NRHS), 1.0, 6.0, ((0, 8), (2, 4)), jnp.float32)
    return {"coupling": coupling, "density": density, "support": support, "loads": loads}


def solve_spd(factor, right):
    half = lax.linalg.triangular_solve(factor, right, left_side=True, lower=True)
    return lax.linalg.triangular_solve(factor, half, left_side=True, lower=True, transpose_a=True)

def batched(left, right):
    return jnp.einsum('lij,ljk->lik', left, right, precision=lax.Precision.HIGHEST)

def reference(coupling, density, support, loads):
    width = coupling.shape[1]
    rho = 0.3 + 0.7 * density.astype(jnp.float32)
    stiff = rho[:, :, None] * coupling * rho[:, None, :]
    zero_block = jnp.zeros_like(stiff[:1])
    below = jnp.concatenate([zero_block, stiff[:-1]], axis=0)
    identity = jnp.eye(width, dtype=jnp.float32)
    diag_block = below + stiff + support[:, :, None] * identity
    lower = -below
    upper = jnp.concatenate([-stiff[:-1], zero_block], axis=0)
    right = loads
    for level in range(LEVELS):
        dist = 2 ** level
        factor = jnp.linalg.cholesky(diag_block)
        solved_lower = solve_spd(factor, lower)
        solved_upper = solve_spd(factor, upper)
        solved_right = solve_spd(factor, right)

        def down(field):
            return jnp.concatenate([jnp.zeros_like(field[:dist]), field[:-dist]], axis=0)

        def rise(field):
            return jnp.concatenate([field[dist:], jnp.zeros_like(field[:dist])], axis=0)
        new_lower = -batched(lower, down(solved_lower))
        new_upper = -batched(upper, rise(solved_upper))
        diag_block = diag_block - batched(lower, down(solved_upper)) - batched(upper, rise(solved_lower))
        right = right - batched(lower, down(solved_right)) - batched(upper, rise(solved_right))
        lower, upper = (new_lower, new_upper)
    return (jnp.swapaxes(diag_block, 1, 2), jnp.swapaxes(lower, 1, 2), jnp.swapaxes(upper, 1, 2), right)
```

```python
import jax
import jax.numpy as jnp
from jax import lax
from jax.experimental import pallas as pl
from jax.experimental.pallas import tpu as pltpu
from jax.sharding import PartitionSpec as P

LEVELS = 2
BLOCK = 128
LEAF = 8
F32 = jnp.float32
BF16 = jnp.bfloat16


def from_behind(shard, axis, by):
    count = lax.axis_size(axis)
    pairs = [(i, i + by) for i in range(count) if 0 <= i + by < count]
    return lax.ppermute(shard, axis, pairs)


def matmul(left, right):
    return jnp.dot(left, right, precision=lax.Precision.HIGH, preferred_element_type=F32)


def leading_matmul(left, right):
    return lax.dot_general(
        left, right, (((0,), (0,)), ((), ())), precision=lax.Precision.HIGH, preferred_element_type=F32
    )


def split(x):
    high = x.astype(BF16)
    return high, (x - high.astype(F32)).astype(BF16)


def dot3(left, right):
    (lh, ll), (rh, rl) = left, right
    dot = lambda a, b: jnp.dot(a, b, preferred_element_type=F32)
    return dot(lh, rh) + (dot(lh, rl) + dot(ll, rh))


def spread(row, j):
    return jnp.broadcast_to(row[:, j : j + 1], row.shape)


def sub(tile, j):
    return jnp.broadcast_to(tile[j : j + 1, :], tile.shape)


def leaf_inverse(columns, rows):
    columns = list(columns)
    for q in range(LEAF):
        here = rows == q
        inv = 1.0 / sub(columns[q], q)
        pivot_column = columns[q]
        for j in range(LEAF):
            if j != q:
                e = sub(columns[j], q) * inv
                columns[j] = jnp.where(here, e, columns[j] - pivot_column * e)
        columns[q] = jnp.where(here, inv, -pivot_column * inv)
    return columns


def block_inverses(blocks):
    count = BLOCK // LEAF
    rows = lax.broadcasted_iota(jnp.int32, (LEAF, BLOCK), 0)
    lanes = lax.broadcasted_iota(jnp.int32, (LEAF, BLOCK), 1)
    tiles = [[b[LEAF * s : LEAF * (s + 1), :] for s in range(count)] for b in blocks]
    for t in range(count):
        base = LEAF * t
        inside = (lanes >= base) & (lanes < base + LEAF)
        unit = (lanes - base == rows).astype(F32)
        for held in tiles:
            row = held[t]
            inverse = leaf_inverse([spread(row, base + j) for j in range(LEAF)], rows)
            framed = jnp.where(inside, unit, row)
            parts = [inverse[j] * sub(framed, j) for j in range(LEAF)]
            while len(parts) > 1:
                parts = [a + b for a, b in zip(parts[::2], parts[1::2])]
            new = parts[0]
            steps = [sub(new, j) for j in range(LEAF)]
            order = list(range(t + 1, count)) + list(range(t))
            for s in order:
                old = held[s]
                total = jnp.where(inside, 0.0, old)
                for j in range(LEAF):
                    total = total - spread(old, base + j) * steps[j]
                held[s] = total
            held[t] = new
    return [jnp.concatenate(held, axis=0) for held in tiles]


def invert_kernel(a_ref, out_ref):
    size = a_ref.shape[0]
    out_ref[...] = a_ref[...]
    unit = (
        lax.broadcasted_iota(jnp.int32, (BLOCK, BLOCK), 0) == lax.broadcasted_iota(jnp.int32, (BLOCK, BLOCK), 1)
    ).astype(F32)

    def step(k, carry):
        here = pl.ds(pl.multiple_of(k * BLOCK, BLOCK), BLOCK)
        (inverse,) = block_inverses([out_ref[here, here]])
        out_ref[here, here] = unit
        row = dot3(split(inverse), split(out_ref[here, :]))
        column = out_ref[:, here]
        out_ref[:, here] = jnp.zeros((size, BLOCK), F32)
        out_ref[...] -= dot3(split(column), split(row))
        out_ref[here, :] = row
        return carry

    lax.fori_loop(0, size // BLOCK, step, 0)


def invert(matrix):
    size = matrix.shape[0]
    return pl.pallas_call(
        invert_kernel,
        out_shape=jax.ShapeDtypeStruct((size, size), F32),
        in_specs=[pl.BlockSpec(memory_space=pltpu.VMEM)],
        out_specs=pl.BlockSpec(memory_space=pltpu.VMEM),
        compiler_params=pltpu.CompilerParams(vmem_limit_bytes=48 * 2**20),
        cost_estimate=pl.CostEstimate(flops=6 * size**3, bytes_accessed=8 * size * size, transcendentals=0),
        name="invert",
    )(matrix)


def shards(coupling, density, support, loads):
    ncols = coupling.shape[1]
    width = coupling.shape[2]
    column_part = lax.axis_index("rhs")
    layer_id = lax.axis_index("layer")
    last_layer = lax.axis_size("layer") - 1
    rho = 0.3 + 0.7 * density[0].astype(F32)
    rho_cols = lax.dynamic_slice_in_dim(rho, column_part * ncols, ncols, 0)
    stiff_t = rho_cols[:, None] * coupling[0] * rho[None, :]
    below_t = from_behind(stiff_t, "layer", 1)
    col_index = lax.broadcasted_iota(jnp.int32, (ncols, width), 0) + column_part * ncols
    row_index = lax.broadcasted_iota(jnp.int32, (ncols, width), 1)
    diag_part = jnp.where(row_index == col_index, support[0][None, :], F32(0.0))
    diag_t = below_t + stiff_t + diag_part
    lower_t = -below_t
    upper_t = jnp.where(layer_id < last_layer, -stiff_t, jnp.zeros_like(stiff_t))
    right = loads[0]
    for level in range(LEVELS):
        dist = 2**level
        full_diag_t, full_lower_t, full_upper_t = (
            lax.all_gather(diag_t, "rhs", axis=0, tiled=True),
            lax.all_gather(lower_t, "rhs", axis=0, tiled=True),
            lax.all_gather(upper_t, "rhs", axis=0, tiled=True),
        )
        inverse = invert(full_diag_t)
        solved_lower = matmul(lower_t, inverse)
        solved_upper = matmul(upper_t, inverse)
        solved_right = matmul(inverse, right)
        low_l, low_u, low_b = from_behind((solved_lower, solved_upper, solved_right), "layer", dist)
        high_l, high_u, high_b = from_behind((solved_lower, solved_upper, solved_right), "layer", -dist)
        new_lower = -matmul(low_l, full_lower_t)
        new_upper = -matmul(high_u, full_upper_t)
        new_diag = diag_t - matmul(low_u, full_lower_t) - matmul(high_l, full_upper_t)
        new_right = right - leading_matmul(full_lower_t, low_b) - leading_matmul(full_upper_t, high_b)
        diag_t, lower_t, upper_t, right = (new_diag, new_lower, new_upper, new_right)
    return (diag_t[None], lower_t[None], upper_t[None], right[None])


def solution(mesh):
    placed = (P("layer", "rhs", None), P("layer", None), P("layer", None), P("layer", None, "rhs"))
    return jax.shard_map(
        shards,
        mesh=mesh,
        in_specs=placed,
        out_specs=(P("layer", "rhs", None),) * 3 + (P("layer", None, "rhs"),),
        check_vma=False,
    )
```

```python
import jax
import jax.numpy as jnp
from jax import lax
from jax.experimental import pallas as pl
from jax.experimental.pallas import tpu as pltpu
from jax.sharding import PartitionSpec as P

BLOCK = 128
LEAF = 8
F32 = jnp.float32
BF16 = jnp.bfloat16


def from_behind(shard, axis, by):
    count = lax.axis_size(axis)
    pairs = [(i, i + by) for i in range(count) if 0 <= i + by < count]
    return lax.ppermute(shard, axis, pairs)


def matmul(left, right):
    return jnp.dot(left, right, precision=lax.Precision.HIGH, preferred_element_type=F32)


def leading_matmul(left, right):
    return lax.dot_general(
        left, right, (((0,), (0,)), ((), ())), precision=lax.Precision.HIGH, preferred_element_type=F32
    )


def split(x):
    high = x.astype(BF16)
    return high, (x - high.astype(F32)).astype(BF16)


def dot3(left, right):
    (lh, ll), (rh, rl) = left, right
    dot = lambda a, b: jnp.dot(a, b, preferred_element_type=F32)
    return dot(lh, rh) + (dot(lh, rl) + dot(ll, rh))


def spread(row, j):
    return jnp.broadcast_to(row[:, j : j + 1], row.shape)


def sub(tile, j):
    return jnp.broadcast_to(tile[j : j + 1, :], tile.shape)


def eliminate(entries, rows):
    held = dict(entries)
    rows = list(rows)
    for q in range(0, LEAF, 2):
        r = q + 1
        a, b, c = held[q, q], held[q, r], held[r, r]
        inv = 1.0 / (a * c - b * b)
        later = range(q + 2, LEAF)
        first = {j: (c * held[q, j] - b * held[r, j]) * inv for j in later}
        second = {j: (a * held[r, j] - b * held[q, j]) * inv for j in later}
        rows[q], rows[r] = (c * rows[q] - b * rows[r]) * inv, (a * rows[r] - b * rows[q]) * inv
        for i in range(LEAF):
            if i in (q, r):
                continue
            x, y = (held[i, q], held[i, r]) if i < q else (held[q, i], held[r, i])
            for j in later:
                if i <= j:
                    held[i, j] = held[i, j] - (x * first[j] + y * second[j])
            rows[i] = rows[i] - (x * rows[q] + y * rows[r])
        for j in later:
            held[q, j], held[r, j] = first[j], second[j]
    return rows


def block_inverses(blocks):
    count = BLOCK // LEAF
    rows = lax.broadcasted_iota(jnp.int32, (LEAF, BLOCK), 0)
    lanes = lax.broadcasted_iota(jnp.int32, (LEAF, BLOCK), 1)
    tiles = [[b[LEAF * s : LEAF * (s + 1), :] for s in range(count)] for b in blocks]
    for t in range(count):
        base = LEAF * t
        inside = (lanes >= base) & (lanes < base + LEAF)
        unit = (lanes - base == rows).astype(F32)
        for held in tiles:
            row = held[t]
            columns = [spread(row, base + j) for j in range(LEAF)]
            entries = {(i, j): sub(columns[j], i) for j in range(LEAF) for i in range(j + 1)}
            framed = jnp.where(inside, unit, row)
            steps = eliminate(entries, [sub(framed, j) for j in range(LEAF)])
            order = list(range(t + 1, count)) + list(range(t))
            for s in order:
                old = held[s]
                total = jnp.where(inside, 0.0, old)
                for j in range(LEAF):
                    total = total - spread(old, base + j) * steps[j]
                held[s] = total
            new = steps[0]
            for j in range(1, LEAF):
                new = jnp.where(rows == j, steps[j], new)
            held[t] = new
    return [jnp.concatenate(held, axis=0) for held in tiles]


def invert_kernel(a_ref, out_ref):
    size = a_ref.shape[0]
    out_ref[...] = a_ref[...]
    unit = (
        lax.broadcasted_iota(jnp.int32, (BLOCK, BLOCK), 0) == lax.broadcasted_iota(jnp.int32, (BLOCK, BLOCK), 1)
    ).astype(F32)

    def step(k, carry):
        here = pl.ds(pl.multiple_of(k * BLOCK, BLOCK), BLOCK)
        (inverse,) = block_inverses([out_ref[here, here]])
        out_ref[here, here] = unit
        row = dot3(split(inverse), split(out_ref[here, :]))
        column = out_ref[:, here]
        out_ref[:, here] = jnp.zeros((size, BLOCK), F32)
        out_ref[...] -= dot3(split(column), split(row))
        out_ref[here, :] = row
        return carry

    lax.fori_loop(0, size // BLOCK, step, 0)


def invert(matrix):
    size = matrix.shape[0]
    return pl.pallas_call(
        invert_kernel,
        out_shape=jax.ShapeDtypeStruct((size, size), F32),
        in_specs=[pl.BlockSpec(memory_space=pltpu.VMEM)],
        out_specs=pl.BlockSpec(memory_space=pltpu.VMEM),
        compiler_params=pltpu.CompilerParams(vmem_limit_bytes=48 * 2**20),
        cost_estimate=pl.CostEstimate(flops=6 * size**3, bytes_accessed=8 * size * size, transcendentals=0),
        name="invert",
    )(matrix)


def gather(slab):
    if lax.axis_size("rhs") != 4:
        return lax.all_gather(slab, "rhs", axis=0, tiled=True)
    swap = lambda x, by: lax.ppermute(x, "rhs", [(i, i ^ by) for i in range(4)])
    part = lax.axis_index("rhs")
    far = swap(slab, 2)
    mate = swap(slab, 1)
    far_mate = swap(far, 1)
    odd, high = part % 2 == 1, part >= 2
    lows = (jnp.where(odd, mate, slab), jnp.where(odd, far_mate, far))
    highs = (jnp.where(odd, slab, mate), jnp.where(odd, far, far_mate))
    pick = lambda pair: (jnp.where(high, pair[1], pair[0]), jnp.where(high, pair[0], pair[1]))
    (first, third), (second, fourth) = pick(lows), pick(highs)
    return jnp.concatenate([first, second, third, fourth], axis=0)


def after(values, *others):
    return lax.optimization_barrier((values, others))[0]


def shards(coupling, density, support, loads):
    ncols = coupling.shape[1]
    width = coupling.shape[2]
    column_part = lax.axis_index("rhs")
    layer_id = lax.axis_index("layer")
    last_layer = lax.axis_size("layer") - 1
    rho = 0.3 + 0.7 * density[0].astype(F32)
    rho_cols = lax.dynamic_slice_in_dim(rho, column_part * ncols, ncols, 0)
    stiff_t = rho_cols[:, None] * coupling[0] * rho[None, :]
    below_t = from_behind(stiff_t, "layer", 1)
    stiff = gather(stiff_t)
    below = gather(below_t)
    col_index = lax.broadcasted_iota(jnp.int32, (ncols, width), 0) + column_part * ncols
    row_index = lax.broadcasted_iota(jnp.int32, (ncols, width), 1)
    diag_t = below_t + stiff_t + jnp.where(row_index == col_index, support[0][None, :], F32(0.0))
    rows = lax.broadcasted_iota(jnp.int32, (width, width), 0)
    columns = lax.broadcasted_iota(jnp.int32, (width, width), 1)
    full_diag = below + stiff + jnp.where(rows == columns, support[0][None, :], F32(0.0))
    above = layer_id < last_layer
    lower_t, full_lower_t = -below_t, -below
    upper_t = jnp.where(above, -stiff_t, jnp.zeros_like(stiff_t))
    full_upper_t = jnp.where(above, -stiff, jnp.zeros_like(stiff))
    right = loads[0]

    inverse = invert(full_diag)
    solved_upper = matmul(upper_t, inverse)
    solved_lower = matmul(lower_t, inverse)
    low_u = from_behind(solved_upper, "layer", 1)
    high_l = from_behind(solved_lower, "layer", -1)
    send_l, send_u = after((solved_lower, solved_upper), low_u, high_l)
    low_l = from_behind(send_l, "layer", 1)
    high_u = from_behind(send_u, "layer", -1)
    diag_t = diag_t - matmul(low_u, full_lower_t) - matmul(high_l, full_upper_t)
    full_diag = gather(diag_t)
    solved_right = matmul(inverse, right)
    send_b = after(solved_right, low_l, high_u)
    low_b = from_behind(send_b, "layer", 1)
    high_b = from_behind(send_b, "layer", -1)
    lower_t, upper_t = -matmul(low_l, full_lower_t), -matmul(high_u, full_upper_t)
    full_diag, lower_t, upper_t = lax.optimization_barrier((full_diag, lower_t, upper_t))
    old_lower_t, old_upper_t = full_lower_t, full_upper_t
    full_lower_t = lax.all_gather(lower_t, "rhs", axis=0, tiled=True)
    full_upper_t = lax.all_gather(upper_t, "rhs", axis=0, tiled=True)

    inverse = invert(full_diag)
    solved = matmul(jnp.concatenate([lower_t, upper_t], axis=0), inverse)
    low = from_behind(solved, "layer", 2)
    high = from_behind(solved, "layer", -2)
    low_b, high_b = after((low_b, high_b), inverse)
    right = right - leading_matmul(old_lower_t, low_b) - leading_matmul(old_upper_t, high_b)
    solved_right = matmul(inverse, right)
    low_b = from_behind(solved_right, "layer", 2)
    high_b = from_behind(solved_right, "layer", -2)
    from_low = matmul(low, full_lower_t)
    from_high = matmul(high, full_upper_t)
    new_lower = -from_low[:ncols]
    new_upper = -from_high[ncols:]
    new_diag = diag_t - from_low[ncols:] - from_high[:ncols]
    right = right - leading_matmul(full_lower_t, low_b) - leading_matmul(full_upper_t, high_b)
    return (new_diag[None], new_lower[None], new_upper[None], right[None])


def solution(mesh):
    placed = (P("layer", "rhs", None), P("layer", None), P("layer", None), P("layer", None, "rhs"))
    return jax.shard_map(
        shards,
        mesh=mesh,
        in_specs=placed,
        out_specs=(P("layer", "rhs", None),) * 3 + (P("layer", None, "rhs"),),
        check_vma=False,
    )
```

```python
import jax
import jax.numpy as jnp
from jax import lax
from jax.experimental import pallas as pl
from jax.experimental.pallas import tpu as pltpu
from jax.sharding import PartitionSpec as P

BLOCK = 128
LEAF = 8
F32 = jnp.float32
BF16 = jnp.bfloat16


def from_behind(shard, axis, by):
    count = lax.axis_size(axis)
    pairs = [(i, i + by) for i in range(count) if 0 <= i + by < count]
    return lax.ppermute(shard, axis, pairs)


def matmul(left, right):
    return jnp.dot(left, right, precision=lax.Precision.HIGH, preferred_element_type=F32)


def leading_matmul(left, right):
    return lax.dot_general(
        left, right, (((0,), (0,)), ((), ())), precision=lax.Precision.HIGH, preferred_element_type=F32
    )


def split(x):
    high = x.astype(BF16)
    return high, (x - high.astype(F32)).astype(BF16)


def dot3(left, right):
    (lh, ll), (rh, rl) = left, right
    dot = lambda a, b: jnp.dot(a, b, preferred_element_type=F32)
    return dot(lh, rh) + (dot(lh, rl) + dot(ll, rh))


def spread(row, j):
    return jnp.broadcast_to(row[:, j : j + 1], row.shape)


def sub(tile, j):
    return jnp.broadcast_to(tile[j : j + 1, :], tile.shape)


def eliminate(entries, rows):
    held = dict(entries)
    rows = list(rows)
    for q in range(0, LEAF, 2):
        r = q + 1
        a, b, c = held[q, q], held[q, r], held[r, r]
        inv = 1.0 / (a * c - b * b)
        later = range(q + 2, LEAF)
        first = {j: (c * held[q, j] - b * held[r, j]) * inv for j in later}
        second = {j: (a * held[r, j] - b * held[q, j]) * inv for j in later}
        rows[q], rows[r] = (c * rows[q] - b * rows[r]) * inv, (a * rows[r] - b * rows[q]) * inv
        for i in range(LEAF):
            if i in (q, r):
                continue
            x, y = (held[i, q], held[i, r]) if i < q else (held[q, i], held[r, i])
            for j in later:
                if i <= j:
                    held[i, j] = held[i, j] - (x * first[j] + y * second[j])
            rows[i] = rows[i] - (x * rows[q] + y * rows[r])
        for j in later:
            held[q, j], held[r, j] = first[j], second[j]
    return rows


def halves(x):
    high = x.astype(BF16).astype(F32)
    return high, x - high


def block_inverses(blocks):
    count = BLOCK // LEAF
    rows = lax.broadcasted_iota(jnp.int32, (LEAF, BLOCK), 0)
    lanes = lax.broadcasted_iota(jnp.int32, (LEAF, BLOCK), 1)
    tiles = [[b[LEAF * s : LEAF * (s + 1), :] for s in range(count)] for b in blocks]
    for t in range(count):
        base = LEAF * t
        inside = (lanes >= base) & (lanes < base + LEAF)
        unit = (lanes - base == rows).astype(F32)
        for held in tiles:
            row = held[t]
            columns = [spread(row, base + j) for j in range(LEAF)]
            entries = {(i, j): sub(columns[j], i) for j in range(LEAF) for i in range(j + 1)}
            framed = jnp.where(inside, unit, row)
            steps = eliminate(entries, [sub(framed, j) for j in range(LEAF)])
            new = steps[0]
            for j in range(1, LEAF):
                new = jnp.where(rows == j, steps[j], new)
            high, low = halves(jnp.where(inside, 0.0, jnp.where(lanes < base, -row, row)))
            new_high, new_low = halves(new)
            update = lax.dot_general(
                jnp.concatenate([high, low, high, low], axis=0).astype(BF16),
                jnp.concatenate([new_high, new_high, new_low, new_low], axis=0).astype(BF16),
                (((0,), (0,)), ((), ())),
                preferred_element_type=F32,
            )
            for s in range(count):
                if s == t:
                    continue
                total = jnp.where(inside, 0.0, held[s])
                if s == t + 1:
                    for j in range(LEAF):
                        total = total - spread(held[s], base + j) * steps[j]
                else:
                    total = total - update[LEAF * s : LEAF * (s + 1), :]
                held[s] = total
            held[t] = new
    return [jnp.concatenate(held, axis=0) for held in tiles]


def invert_kernel(a_ref, out_ref):
    size = a_ref.shape[0]
    out_ref[...] = a_ref[...]
    unit = (
        lax.broadcasted_iota(jnp.int32, (BLOCK, BLOCK), 0) == lax.broadcasted_iota(jnp.int32, (BLOCK, BLOCK), 1)
    ).astype(F32)

    def step(k, carry):
        here = pl.ds(pl.multiple_of(k * BLOCK, BLOCK), BLOCK)
        (inverse,) = block_inverses([out_ref[here, here]])
        out_ref[here, here] = unit
        row = dot3(split(inverse), split(out_ref[here, :]))
        column = out_ref[:, here]
        out_ref[:, here] = jnp.zeros((size, BLOCK), F32)
        out_ref[...] -= dot3(split(column), split(row))
        out_ref[here, :] = row
        return carry

    lax.fori_loop(0, size // BLOCK, step, 0)


def invert(matrix):
    size = matrix.shape[0]
    return pl.pallas_call(
        invert_kernel,
        out_shape=jax.ShapeDtypeStruct((size, size), F32),
        in_specs=[pl.BlockSpec(memory_space=pltpu.VMEM)],
        out_specs=pl.BlockSpec(memory_space=pltpu.VMEM),
        compiler_params=pltpu.CompilerParams(vmem_limit_bytes=48 * 2**20),
        cost_estimate=pl.CostEstimate(flops=6 * size**3, bytes_accessed=8 * size * size, transcendentals=0),
        name="invert",
    )(matrix)


def gather(slab):
    if lax.axis_size("rhs") != 4:
        return lax.all_gather(slab, "rhs", axis=0, tiled=True)
    swap = lambda x, by: lax.ppermute(x, "rhs", [(i, i ^ by) for i in range(4)])
    part = lax.axis_index("rhs")
    far = swap(slab, 2)
    mate = swap(slab, 1)
    far_mate = swap(far, 1)
    odd, high = part % 2 == 1, part >= 2
    lows = (jnp.where(odd, mate, slab), jnp.where(odd, far_mate, far))
    highs = (jnp.where(odd, slab, mate), jnp.where(odd, far, far_mate))
    pick = lambda pair: (jnp.where(high, pair[1], pair[0]), jnp.where(high, pair[0], pair[1]))
    (first, third), (second, fourth) = pick(lows), pick(highs)
    return jnp.concatenate([first, second, third, fourth], axis=0)


def after(values, *others):
    return lax.optimization_barrier((values, others))[0]


def shards(coupling, density, support, loads):
    ncols = coupling.shape[1]
    width = coupling.shape[2]
    column_part = lax.axis_index("rhs")
    layer_id = lax.axis_index("layer")
    last_layer = lax.axis_size("layer") - 1
    rho = 0.3 + 0.7 * density[0].astype(F32)
    rho_cols = lax.dynamic_slice_in_dim(rho, column_part * ncols, ncols, 0)
    stiff_t = rho_cols[:, None] * coupling[0] * rho[None, :]
    below_t = from_behind(stiff_t, "layer", 1)
    stiff = gather(stiff_t)
    below = gather(below_t)
    col_index = lax.broadcasted_iota(jnp.int32, (ncols, width), 0) + column_part * ncols
    row_index = lax.broadcasted_iota(jnp.int32, (ncols, width), 1)
    diag_t = below_t + stiff_t + jnp.where(row_index == col_index, support[0][None, :], F32(0.0))
    rows = lax.broadcasted_iota(jnp.int32, (width, width), 0)
    columns = lax.broadcasted_iota(jnp.int32, (width, width), 1)
    full_diag = below + stiff + jnp.where(rows == columns, support[0][None, :], F32(0.0))
    above = layer_id < last_layer
    lower_t, full_lower_t = -below_t, -below
    upper_t = jnp.where(above, -stiff_t, jnp.zeros_like(stiff_t))
    full_upper_t = jnp.where(above, -stiff, jnp.zeros_like(stiff))
    right = loads[0]

    inverse = invert(full_diag)
    solved_upper = matmul(upper_t, inverse)
    solved_lower = matmul(lower_t, inverse)
    low_u = from_behind(solved_upper, "layer", 1)
    high_l = from_behind(solved_lower, "layer", -1)
    send_l, send_u = after((solved_lower, solved_upper), low_u, high_l)
    low_l = from_behind(send_l, "layer", 1)
    high_u = from_behind(send_u, "layer", -1)
    diag_t = diag_t - matmul(low_u, full_lower_t) - matmul(high_l, full_upper_t)
    full_diag = gather(diag_t)
    solved_right = matmul(inverse, right)
    send_b = after(solved_right, low_l, high_u)
    low_b = from_behind(send_b, "layer", 1)
    high_b = from_behind(send_b, "layer", -1)
    lower_t, upper_t = -matmul(low_l, full_lower_t), -matmul(high_u, full_upper_t)
    full_diag, lower_t, upper_t = lax.optimization_barrier((full_diag, lower_t, upper_t))
    old_lower_t, old_upper_t = full_lower_t, full_upper_t
    full_lower_t = lax.all_gather(lower_t, "rhs", axis=0, tiled=True)
    full_upper_t = lax.all_gather(upper_t, "rhs", axis=0, tiled=True)

    inverse = invert(full_diag)
    solved = matmul(jnp.concatenate([lower_t, upper_t], axis=0), inverse)
    low = from_behind(solved, "layer", 2)
    high = from_behind(solved, "layer", -2)
    low_b, high_b = after((low_b, high_b), inverse)
    right = right - leading_matmul(old_lower_t, low_b) - leading_matmul(old_upper_t, high_b)
    solved_right = matmul(inverse, right)
    low_b = from_behind(solved_right, "layer", 2)
    high_b = from_behind(solved_right, "layer", -2)
    from_low = matmul(low, full_lower_t)
    from_high = matmul(high, full_upper_t)
    new_lower = -from_low[:ncols]
    new_upper = -from_high[ncols:]
    new_diag = diag_t - from_low[ncols:] - from_high[:ncols]
    right = right - leading_matmul(full_lower_t, low_b) - leading_matmul(full_upper_t, high_b)
    return (new_diag[None], new_lower[None], new_upper[None], right[None])


def solution(mesh):
    placed = (P("layer", "rhs", None), P("layer", None), P("layer", None), P("layer", None, "rhs"))
    return jax.shard_map(
        shards,
        mesh=mesh,
        in_specs=placed,
        out_specs=(P("layer", "rhs", None),) * 3 + (P("layer", None, "rhs"),),
        check_vma=False,
    )
```
